128 devices in a mesh: row: 16 (over z_hi, x, core), col: 8 (over z_lo, y).
Axes of the slice: x: 4, y: 4, z: 4 (z_hi: 2, z_lo: 2; z = z_hi * 2 + z_lo), core: 2. Of those that a mesh axis runs over, the one named last changes fastest.
Arguments:
- doubles: bfloat16 [3600, 3840], P('row', 'col'), may hold values from -6 to 6
- singles: float32 [60, 480], replicated, may hold values from -3 to 3
- integrals: bfloat16 [3840, 32768], P(None, ('col', 'row')), may hold values from -0.09375 to 0.09375
Outputs:
- ladder: bfloat16 [3600, 32768], P('row', 'col')
The draws below stay inside these ranges and needn't reach their ends.
All inputs are finite; a program needn't handle non-finite values.
Results may differ from the reference program's by a relative error of at most 0.005.
Values may be sent and summed in bfloat16 or wider, within the bound.
A program may use at most 128 MiB of HBM per device.

```python
import jax
import jax.numpy as jnp

O = 60
V = 480
CWIN = 8
OO = 3600
K = 3840
NAB = 32768


def level_of(rng, dims, shards, low, largest):
    def one(axis_at, parts):
        draws = jax.random.uniform(jax.random.fold_in(jax.random.fold_in(rng, 6), axis_at), (parts,), jnp.float32, low / len(shards), largest / len(shards))
        return jnp.repeat(jnp.exp(draws), dims[axis_at] // parts).reshape((-1,) + (1,) * (len(dims) - axis_at - 1))

    gain = one(*shards[0])
    for cut in shards[1:]:
        gain = gain * one(*cut)
    return gain


def noise(own_key, dims, width, most, pieces=(), held_as=jnp.bfloat16):
    gain = level_of(own_key, dims, pieces, -0.22, 0.18) if pieces else 1.0
    result = jax.random.normal(own_key, dims, jnp.float32) * width * gain
    return jnp.minimum(jnp.maximum(result, -most), most).astype(held_as)


def setup_inputs(seed: int = 0) -> dict:
    keys = jax.random.split(jax.random.key(seed), 4)
    doubles = noise(keys[0], (OO, K), 1.0, 6.0, ((0, 16), (1, 8)))
    singles = noise(keys[1], (O, V), 0.5, 3.0, (), jnp.float32)
    integrals = noise(keys[2], (K, NAB), K ** -0.5, 0.09375, ((1, 128),))
    return dict(doubles=doubles, singles=singles, integrals=integrals)


def reference(doubles, singles, integrals):
    window = singles[:, :CWIN]
    product = (window[:, None, :, None] * singles[None, :, None, :]).reshape(OO, K)
    tau = (doubles.astype(jnp.float32) + product).astype(jnp.bfloat16)
    return jnp.dot(tau, integrals, preferred_element_type=jnp.float32).astype(jnp.bfloat16)
```

```python
import functools

import jax
import jax.numpy as jnp
from jax import lax
from jax.experimental import pallas as pl
from jax.experimental.pallas import tpu as pltpu
from jax.sharding import PartitionSpec as P

MESH = pl.DeviceIdType.MESH
ROWS = 240
CUT = 176
DEPTH = 480
WIDTH = 256
ALL = (0, ROWS)
FIRST = (0, CUT)
SECOND = (CUT, ROWS)
HALVES = {FIRST: ((0, 96), (96, CUT)), SECOND: ((CUT, 208), (208, ROWS))}


def span(rows):
    return pl.ds(rows[0], rows[1] - rows[0])


def build_tau(doubles, singles):
    pair_rows, pair_cols = doubles.shape
    occupied = singles.shape[0]
    row, col = lax.axis_index("row"), lax.axis_index("col")
    pairs = occupied * occupied
    tiled = jnp.tile(singles, (pair_rows // occupied + 2, 1))
    right = lax.dynamic_slice(tiled, (lax.rem(row * pair_rows, occupied), 0), (pair_rows, pair_cols))
    column = lax.dynamic_slice(singles, (0, col), (occupied, 1))
    every = jnp.broadcast_to(column, (occupied, occupied)).reshape(pairs)
    left = lax.dynamic_slice(every, (row * pair_rows,), (pair_rows,))
    tau = doubles.astype(jnp.float32) + left[:, None] * right
    return jnp.pad(tau, ((0, ROWS - pair_rows), (0, 0))).astype(jnp.bfloat16)


def kernel(tau_ref, b_ref, out_ref, a, b, c, send_sem, recv_sem, local_sem):
    row, col = lax.axis_index("row"), lax.axis_index("col")
    zh, x, core = row // 8, lax.rem(row // 2, 4), lax.rem(row, 2)
    zl, y = col // 4, lax.rem(col, 4)
    zo = 1 - zl

    def at(dx=0, dy=0, dh=0, dl=0, dc=0):
        return (
            lax.rem(zh + dh, 2) * 8 + lax.rem(x + dx, 4) * 2 + lax.rem(core + dc, 2),
            lax.rem(zl + dl, 2) * 4 + lax.rem(y + dy, 4),
        )

    xs = [lax.rem(x + d, 4) for d in range(4)]
    ys = [lax.rem(y + d, 4) for d in range(4)]
    peers = [at(dx=1), at(dx=2), at(dx=3), at(dy=1), at(dy=3), at(dl=1), at(dh=1), at(dc=1)]

    barrier = pltpu.get_barrier_semaphore()
    for peer in peers:
        pl.semaphore_signal(barrier, inc=1, device_id=peer, device_id_type=MESH)
    pl.semaphore_wait(barrier, len(peers))

    copies = []

    def send(src, dst, device):
        number = len(copies)
        copy = pltpu.make_async_remote_copy(
            src_ref=src,
            dst_ref=dst,
            send_sem=send_sem.at[number],
            recv_sem=recv_sem.at[number],
            device_id=device,
            device_id_type=MESH,
        )
        copy.start()
        copies.append(copy)
        return copy

    def send_a(index, rows, device):
        ref = a.at[index + (span(rows),)]
        return send(ref, ref, device)

    def y_start(dx, lo, rows):
        index = (xs[dx], ys[0], lo)
        return [send_a(index, rows, at(dy=1)), send_a(index, rows, at(dy=3))]

    def y_pass(started, dx, lo, rows, flip):
        up, down = HALVES[rows][::-1] if flip else HALVES[rows]
        for copy in started:
            copy.wait_recv()
        return [
            send_a((xs[dx], ys[3], lo), up, at(dy=1)),
            send_a((xs[dx], ys[1], lo), down, at(dy=3)),
        ]

    def x_start(dy, lo, rows):
        index = (xs[0], ys[dy], lo)
        return [send_a(index, rows, at(dx=1)), send_a(index, rows, at(dx=3))]

    def x_pass(started, dy, lo, rows, flip):
        up, down = HALVES[rows][::-1] if flip else HALVES[rows]
        for copy in started:
            copy.wait_recv()
        return [
            send_a((xs[3], ys[dy], lo), up, at(dx=1)),
            send_a((xs[1], ys[dy], lo), down, at(dx=3)),
        ]

    def arrive(started):
        for copy in started:
            copy.wait_recv()

    both = pl.ds(0, 2)

    def product(dx, half, q):
        total = None
        for lo in range(2):
            for yy in range(4):
                term = jnp.dot(
                    a[xs[dx], yy, lo],
                    b[half, q, pl.ds((lo * 4 + yy) * DEPTH, DEPTH), :],
                    preferred_element_type=jnp.float32,
                )
                total = term if total is None else total + term
        c[dx, half * 2 + q] = total.astype(jnp.bfloat16)

    def own_columns(dx):
        @pl.loop(0, 2)
        def _(q):
            product(dx, 0, q)

    def other_columns(dx, q):
        product(dx, 1, q)

    results = []

    def place(half, q, count):
        return out_ref.at[pl.ds(lax.rem(zh + half, 2) * 8 + x * 2 + q, count)]

    def send_c(dx, half, q, count):
        src = c.at[dx, pl.ds(half * 2 + q, count)]
        results.append(send(src, place(half, q, count), at(dx=dx)))

    mine = pltpu.make_async_copy(b_ref, b.at[0, core], local_sem.at[0])
    mine.start()
    sibling = send(b_ref, b.at[0, core], at(dc=1))

    a[x, y, zl] = tau_ref[...]
    pair = send_a((xs[0], ys[0], zl), ALL, at(dl=1))
    x_o = x_start(0, zl, FIRST)
    y_0o = y_start(0, zl, FIRST)
    y_so = y_start(0, zl, SECOND)

    depth = b.shape[2] // 2
    part = pl.ds(pl.multiple_of(core * depth, depth), depth)
    mine.wait()
    sibling.wait_recv()
    columns = [send(b.at[0, 0, part], b.at[1, 0, part], at(dh=1))]

    x_o2 = x_pass(x_o, 0, zl, FIRST, False)
    pair.wait_recv()
    x_p = x_start(0, zo, FIRST)
    y_sp = y_start(0, zo, SECOND)
    y_0o2 = y_pass(y_0o, 0, zl, FIRST, False)
    y_so2 = y_pass(y_so, 0, zl, SECOND, False)
    arrive(x_o2)
    y_2o = y_start(2, zl, FIRST)
    x_p2 = x_pass(x_p, 0, zo, FIRST, True)
    y_sp2 = y_pass(y_sp, 0, zo, SECOND, True)
    x_s = {}
    x_s[0, 0] = x_start(0, zl, SECOND)
    x_s[0, 1] = x_start(0, zo, SECOND)
    arrive(x_p2)
    y_2p = y_start(2, zo, FIRST)
    x_t = {}
    x_t[0, 0] = x_pass(x_s[0, 0], 0, zl, SECOND, False)
    x_t[0, 1] = x_pass(x_s[0, 1], 0, zo, SECOND, True)
    for dy in (1, 3):
        x_s[dy, 0] = x_start(dy, zl, SECOND)
        x_s[dy, 1] = x_start(dy, zo, SECOND)
    y_2o2 = y_pass(y_2o, 2, zl, FIRST, False)
    y_1o = y_start(1, zl, FIRST)
    for dy in (1, 3):
        x_t[dy, 0] = x_pass(x_s[dy, 0], dy, zl, SECOND, False)
        x_t[dy, 1] = x_pass(x_s[dy, 1], dy, zo, SECOND, True)
    arrive(y_so2 + y_sp2)
    x_s[2, 0] = x_start(2, zl, SECOND)
    x_s[2, 1] = x_start(2, zo, SECOND)
    y_2p2 = y_pass(y_2p, 2, zo, FIRST, True)
    y_1p = y_start(1, zo, FIRST)
    x_t[2, 0] = x_pass(x_s[2, 0], 2, zl, SECOND, False)
    x_t[2, 1] = x_pass(x_s[2, 1], 2, zo, SECOND, True)

    columns[0].wait_recv()
    columns.append(send(b.at[0, 1, part], b.at[1, 1, part], at(dh=1)))
    shared = [send(b.at[1, 0, part], b.at[1, 0, part], at(dc=1))]

    y_1o2 = y_pass(y_1o, 1, zl, FIRST, False)
    y_3o = y_start(3, zl, FIRST)
    for key in x_t:
        arrive(x_t[key])
    arrive(y_2o2 + y_2p2)
    own_columns(2)
    send_c(2, 0, 0, 2)
    y_1p2 = y_pass(y_1p, 1, zo, FIRST, True)
    y_3p = y_start(3, zo, FIRST)
    shared[0].wait_recv()
    other_columns(2, 0)
    send_c(2, 1, 0, 1)
    y_3o2 = y_pass(y_3o, 3, zl, FIRST, False)
    y_0p = y_start(0, zo, FIRST)
    arrive(y_1o2 + y_1p2)
    own_columns(1)
    send_c(1, 0, 0, 2)
    other_columns(1, 0)
    send_c(1, 1, 0, 1)
    y_3p2 = y_pass(y_3p, 3, zo, FIRST, True)
    y_0p2 = y_pass(y_0p, 0, zo, FIRST, True)
    columns[1].wait_recv()
    shared.append(send(b.at[1, 1, part], b.at[1, 1, part], at(dc=1)))
    arrive(y_3o2 + y_3p2)
    own_columns(3)
    send_c(3, 0, 0, 2)
    other_columns(3, 0)
    send_c(3, 1, 0, 1)
    shared[1].wait_recv()
    for dx in (2, 3, 1):
        other_columns(dx, 1)
        send_c(dx, 1, 1, 1)
    arrive(y_0o2 + y_0p2)
    own_columns(0)
    other_columns(0, 0)
    other_columns(0, 1)
    kept = [
        pltpu.make_async_copy(c.at[0, pl.ds(half * 2, 2)], place(half, 0, 2), local_sem.at[1 + half])
        for half in range(2)
    ]
    for copy in kept:
        copy.start()
    for copy in kept:
        copy.wait()
    for copy in results:
        copy.wait_recv()
    for copy in copies:
        copy.wait_send()


def on_device(doubles, singles, integrals):
    rows = doubles.shape[0]
    depth, width = integrals.shape
    blocks = pl.pallas_call(
        kernel,
        out_shape=jax.ShapeDtypeStruct((16, ROWS, width), jnp.bfloat16),
        in_specs=[pl.BlockSpec(memory_space=pltpu.VMEM), pl.BlockSpec(memory_space=pl.ANY)],
        out_specs=pl.BlockSpec(memory_space=pl.ANY),
        scratch_shapes=[
            pltpu.VMEM((4, 4, 2, ROWS, DEPTH), jnp.bfloat16),
            pltpu.VMEM((2, 2, depth, width), jnp.bfloat16),
            pltpu.VMEM((4, 4, ROWS, width), jnp.bfloat16),
            pltpu.SemaphoreType.DMA((128,)),
            pltpu.SemaphoreType.DMA((128,)),
            pltpu.SemaphoreType.DMA((3,)),
        ],
        compiler_params=pltpu.CompilerParams(
            collective_id=0, has_side_effects=True, vmem_limit_bytes=48 << 20
        ),
        cost_estimate=pl.CostEstimate(
            flops=2 * rows * depth * 16 * width, bytes_accessed=32 << 20, transcendentals=0
        ),
        name="ladder",
    )(build_tau(doubles, singles), integrals)
    return blocks[:, :rows].transpose(1, 0, 2).reshape(rows, 16 * width)


def solution(mesh):
    return jax.shard_map(
        on_device,
        mesh=mesh,
        in_specs=(P("row", "col"), P(), P(None, ("col", "row"))),
        out_specs=P("row", "col"),
        check_vma=False,
    )
```

```python
import math

import jax
import jax.numpy as jnp
from jax import lax
from jax.experimental import pallas as pl
from jax.experimental.pallas import tpu as pltpu
from jax.sharding import PartitionSpec as P

MESH = pl.DeviceIdType.MESH
ROWS = 240
CUT = 176
DEPTH = 480
WIDTH = 256
ALL = (0, ROWS)
FIRST = (0, CUT)
SECOND = (CUT, ROWS)
HALVES = {FIRST: ((0, 96), (96, CUT)), SECOND: ((CUT, 208), (208, ROWS))}


def span(rows):
    return pl.ds(rows[0], rows[1] - rows[0])


def kernel(doubles_hbm, singles_hbm, b_ref, out_ref, a, own, other, c, outer, doubles_ref, singles_ref, send_sem, recv_sem, local_sem):
    row, col = lax.axis_index("row"), lax.axis_index("col")
    zh, x, core = row // 8, lax.rem(row // 2, 4), lax.rem(row, 2)
    zl, y = col // 4, lax.rem(col, 4)
    zo = 1 - zl

    def at(dx=0, dy=0, dh=0, dl=0, dc=0):
        return (
            lax.rem(zh + dh, 2) * 8 + lax.rem(x + dx, 4) * 2 + lax.rem(core + dc, 2),
            lax.rem(zl + dl, 2) * 4 + lax.rem(y + dy, 4),
        )

    xs = [lax.rem(x + d, 4) for d in range(4)]
    ys = [lax.rem(y + d, 4) for d in range(4)]
    peers = [at(dx=1), at(dx=2), at(dx=3), at(dy=1), at(dy=3), at(dl=1), at(dh=1), at(dc=1)]

    bring = [
        pltpu.make_async_copy(doubles_hbm, doubles_ref, local_sem.at[14]),
        pltpu.make_async_copy(singles_hbm, singles_ref, local_sem.at[15]),
    ]
    for copy in bring[::-1]:
        copy.start()
    barrier = pltpu.get_barrier_semaphore()
    for peer in peers:
        pl.semaphore_signal(barrier, inc=1, device_id=peer, device_id_type=MESH)

    mine = pltpu.make_async_copy(b_ref, own.at[core], local_sem.at[0])
    mine.start()

    pairs, depth = doubles_ref.shape
    occupied = singles_ref.shape[0]
    first = (row * pairs) // occupied
    skip = lax.rem(row * pairs, occupied)
    lanes = lax.broadcasted_iota(jnp.int32, (1, depth), 1)
    bring[1].wait()
    for g in range(outer.shape[0] // occupied):
        line = singles_ref[pl.ds(jnp.minimum(first + g, occupied - 1), 1), :]
        factor = jnp.sum(jnp.where(lanes == col, line, 0.0), axis=1, keepdims=True)
        outer[pl.ds(g * occupied, occupied), :] = singles_ref[...] * factor
    bring[0].wait()
    a[x, y, zl, pl.ds(ROWS - 16, 16), :] = jnp.zeros((16, depth), jnp.bfloat16)
    for offset in range(0, occupied, math.gcd(pairs, occupied)):

        @pl.when(skip == offset)
        def _(offset=offset):
            tau = doubles_ref[...].astype(jnp.float32) + outer[pl.ds(offset, pairs), :]
            a[x, y, zl, pl.ds(0, pairs), :] = tau.astype(jnp.bfloat16)


    pl.semaphore_wait(barrier, len(peers))

    copies = []

    def send(src, dst, device):
        number = len(copies)
        copy = pltpu.make_async_remote_copy(
            src_ref=src,
            dst_ref=dst,
            send_sem=send_sem.at[number],
            recv_sem=recv_sem.at[number],
            device_id=device,
            device_id_type=MESH,
        )
        copy.start()
        copies.append(copy)
        return copy

    def send_a(index, rows, device):
        ref = a.at[index + (span(rows),)]
        return send(ref, ref, device)

    def arrive(started):
        for copy in started:
            copy.wait_recv()

    def y_start(dx, lo, rows):
        index = (xs[dx], ys[0], lo)
        return [send_a(index, rows, at(dy=1)), send_a(index, rows, at(dy=3))]

    def y_pass(started, dx, lo, rows, flip):
        up, down = HALVES[rows][::-1] if flip else HALVES[rows]
        arrive(started)
        return [
            send_a((xs[dx], ys[3], lo), up, at(dy=1)),
            send_a((xs[dx], ys[1], lo), down, at(dy=3)),
        ]

    def x_start(dy, lo, rows):
        index = (xs[0], ys[dy], lo)
        return [send_a(index, rows, at(dx=1)), send_a(index, rows, at(dx=3))]

    def x_pass(started, dy, lo, rows, flip):
        up, down = HALVES[rows][::-1] if flip else HALVES[rows]
        arrive(started)
        return [
            send_a((xs[3], ys[dy], lo), up, at(dx=1)),
            send_a((xs[1], ys[dy], lo), down, at(dx=3)),
        ]

    def product(left, right, where, cols):
        total = None
        for lo in range(2):
            for yy in range(4):
                term = jnp.dot(
                    left(yy, lo),
                    right[pl.ds((lo * 4 + yy) * DEPTH, DEPTH), :],
                    preferred_element_type=jnp.float32,
                )
                total = term if total is None else total + term
        total = total.astype(jnp.bfloat16)
        at_row = 0
        for dx, rows in where:
            count = rows[1] - rows[0]
            c[dx, span(rows), cols] = total[at_row : at_row + count]
            at_row += count

    def block(which, q, j=None):
        ref = which.at[q]
        return ref if j is None else ref.at[:, pl.ds(j * 128, 128)]

    def first_rows(dx, right, cols):
        product(lambda yy, lo: a[xs[dx], yy, lo, span(FIRST)], right, [(dx, FIRST)], cols)

    def second_rows(right, cols):
        product(
            lambda yy, lo: jnp.concatenate([a[xs[d], yy, lo, span(SECOND)] for d in range(4)], axis=0),
            right,
            [(d, SECOND) for d in range(4)],
            cols,
        )

    results = []
    kept = []

    def send_c(dx, rows, half, start, count):
        base = (lax.rem(zh + half, 2) * 8 + x * 2) * WIDTH + start
        dst = out_ref.at[span(rows), pl.ds(pl.multiple_of(base, 128), count)]
        src = c.at[dx, span(rows), pl.ds(half * 512 + start, count)]
        if dx:
            results.append(send(src, dst, at(dx=dx)))
        else:
            copy = pltpu.make_async_copy(src, dst, local_sem.at[1 + len(kept)])
            copy.start()
            kept.append(copy)

    def own_first(dx):
        @pl.loop(0, 2)
        def _(q):
            first_rows(dx, own.at[q], pl.ds(pl.multiple_of(q * WIDTH, WIDTH), WIDTH))

        send_c(dx, FIRST, 0, 0, 512)

    def other_first(dx, q, j=None):
        start, count = (q * 256, 256) if j is None else (q * 256 + j * 128, 128)
        first_rows(dx, block(other, q, j), pl.ds(512 + start, count))
        send_c(dx, FIRST, 1, start, count)

    def own_second():
        @pl.loop(0, 2)
        def _(q):
            second_rows(own.at[q], pl.ds(pl.multiple_of(q * WIDTH, WIDTH), WIDTH))

        for dx in (2, 1, 3, 0):
            send_c(dx, SECOND, 0, 0, 512)

    def other_second(q, j=None):
        start, count = (q * 256, 256) if j is None else (q * 256 + j * 128, 128)
        second_rows(block(other, q, j), pl.ds(512 + start, count))
        for dx in (2, 1, 3, 0):
            send_c(dx, SECOND, 1, start, count)

    half = own.shape[1] // 2
    part = pl.ds(pl.multiple_of(core * half, half), half)
    lane_block = {None: pl.ds(0, WIDTH), 0: pl.ds(0, 128), 1: pl.ds(128, 128)}

    def across(q, j):
        return send(own.at[q, part, lane_block[j]], other.at[q, part, lane_block[j]], at(dh=1))

    def share(started, q, j):
        started.wait_recv()
        ref = other.at[q, part, lane_block[j]]
        return send(ref, ref, at(dc=1))

    o, p = zl, zo
    pair = [send_a((xs[0], ys[0], zl), FIRST, at(dl=1)), send_a((xs[0], ys[0], zl), SECOND, at(dl=1))]
    sibling = send(b_ref, own.at[core], at(dc=1))
    xf = {}
    yf = {}
    x_o = x_start(0, o, FIRST)
    y_so = y_start(0, o, SECOND)
    y_0o = y_start(0, o, FIRST)
    xs_ = {}
    xt = {}
    xs_[0, 0] = x_start(0, o, SECOND)
    y_so2 = y_pass(y_so, 0, o, SECOND, False)
    mine.wait()
    sibling.wait_recv()
    za = across(0, None)
    x_o2 = x_pass(x_o, 0, o, FIRST, False)
    y_1o = y_start(1, o, FIRST)
    arrive(pair)
    x_p = x_start(0, p, FIRST)
    y_sp = y_start(0, p, SECOND)
    zb = across(1, 0)
    zc = across(1, 1)
    y_0o2 = y_pass(y_0o, 0, o, FIRST, False)
    xt[0, 0] = x_pass(xs_[0, 0], 0, o, SECOND, False)
    xs_[0, 1] = x_start(0, p, SECOND)
    arrive(x_o2)
    y_2o = y_start(2, o, FIRST)
    xs_[1, 0] = x_start(1, o, SECOND)
    xs_[3, 0] = x_start(3, o, SECOND)
    y_1o2 = y_pass(y_1o, 1, o, FIRST, False)
    x_p2 = x_pass(x_p, 0, p, FIRST, True)
    y_sp2 = y_pass(y_sp, 0, p, SECOND, True)
    xt[0, 1] = x_pass(xs_[0, 1], 0, p, SECOND, True)
    xs_[1, 1] = x_start(1, p, SECOND)
    xs_[3, 1] = x_start(3, p, SECOND)
    xt[1, 0] = x_pass(xs_[1, 0], 1, o, SECOND, False)
    xt[3, 0] = x_pass(xs_[3, 0], 3, o, SECOND, False)
    arrive(x_p2)
    y_2p = y_start(2, p, FIRST)
    y_2o2 = y_pass(y_2o, 2, o, FIRST, False)
    arrive(y_so2)
    xs_[2, 0] = x_start(2, o, SECOND)
    y_1p = y_start(1, p, FIRST)
    xt[1, 1] = x_pass(xs_[1, 1], 1, p, SECOND, True)
    xt[3, 1] = x_pass(xs_[3, 1], 3, p, SECOND, True)
    arrive(y_sp2)
    xs_[2, 1] = x_start(2, p, SECOND)
    y_2p2 = y_pass(y_2p, 2, p, FIRST, True)
    y_3o = y_start(3, o, FIRST)
    xt[2, 0] = x_pass(xs_[2, 0], 2, o, SECOND, False)
    xt[2, 1] = x_pass(xs_[2, 1], 2, p, SECOND, True)
    sa = share(za, 0, None)
    y_1p2 = y_pass(y_1p, 1, p, FIRST, True)
    y_3p = y_start(3, p, FIRST)
    for key in xt:
        arrive(xt[key])
    own_second()
    arrive(y_2o2 + y_2p2)
    own_first(2)
    sa.wait_recv()
    other_second(0)
    other_first(2, 0)
    y_3o2 = y_pass(y_3o, 3, o, FIRST, False)
    arrive(y_1o2 + y_1p2)
    own_first(1)
    other_first(1, 0)
    sb = share(zb, 1, 0)
    y_3p2 = y_pass(y_3p, 3, p, FIRST, True)
    y_0p = y_start(0, p, FIRST)
    sb.wait_recv()
    other_second(1, 0)
    other_first(2, 1, 0)
    other_first(1, 1, 0)
    arrive(y_3o2 + y_3p2)
    own_first(3)
    other_first(3, 0)
    other_first(3, 1, 0)
    y_0p2 = y_pass(y_0p, 0, p, FIRST, True)
    sc = share(zc, 1, 1)
    sc.wait_recv()
    other_first(3, 1, 1)
    other_second(1, 1)
    other_first(2, 1, 1)
    other_first(1, 1, 1)
    arrive(y_0o2 + y_0p2)
    own_first(0)
    other_first(0, 0)
    other_first(0, 1, 0)
    other_first(0, 1, 1)
    for copy in kept:
        copy.wait()
    arrive(results)
    for copy in copies:
        copy.wait_send()


def on_device(doubles, singles, integrals):
    rows = doubles.shape[0]
    depth, width = integrals.shape
    padded = pl.pallas_call(
        kernel,
        out_shape=jax.ShapeDtypeStruct((ROWS, 16 * width), jnp.bfloat16),
        in_specs=[
            pl.BlockSpec(memory_space=pltpu.HBM),
            pl.BlockSpec(memory_space=pltpu.HBM),
            pl.BlockSpec(memory_space=pltpu.HBM),
        ],
        out_specs=pl.BlockSpec(memory_space=pl.ANY),
        scratch_shapes=[
            pltpu.VMEM((4, 4, 2, ROWS, DEPTH), jnp.bfloat16),
            pltpu.VMEM((2, depth, width), jnp.bfloat16),
            pltpu.VMEM((2, depth, width), jnp.bfloat16),
            pltpu.VMEM((4, ROWS, 4 * width), jnp.bfloat16),
            pltpu.VMEM((300, DEPTH), jnp.float32),
            pltpu.VMEM(doubles.shape, doubles.dtype),
            pltpu.VMEM(singles.shape, singles.dtype),
            pltpu.SemaphoreType.DMA((128,)),
            pltpu.SemaphoreType.DMA((128,)),
            pltpu.SemaphoreType.DMA((16,)),
        ],
        compiler_params=pltpu.CompilerParams(
            collective_id=0, has_side_effects=True, vmem_limit_bytes=60 << 20
        ),
        cost_estimate=pl.CostEstimate(
            flops=2 * rows * depth * 16 * width, bytes_accessed=32 << 20, transcendentals=0
        ),
        name="ladder",
    )(doubles, singles, integrals)
    return padded[:rows]


def solution(mesh):
    return jax.shard_map(
        on_device,
        mesh=mesh,
        in_specs=(P("row", "col"), P(), P(None, ("col", "row"))),
        out_specs=P("row", "col"),
        check_vma=False,
    )
```

```python
import math

import jax
import jax.numpy as jnp
from jax import lax
from jax.experimental import pallas as pl
from jax.experimental.pallas import tpu as pltpu
from jax.sharding import PartitionSpec as P

MESH = pl.DeviceIdType.MESH
ROWS = 240
CUT = 176
DEPTH = 480
WIDTH = 256
ALL = (0, ROWS)
FIRST = (0, CUT)
SECOND = (CUT, ROWS)
EARLY = (0, 96)
LATE = (96, CUT)
HALVES = {
    FIRST: ((0, 96), (96, CUT)),
    SECOND: ((CUT, 208), (208, ROWS)),
    EARLY: ((0, 48), (48, 96)),
    LATE: ((96, 144), (144, CUT)),
}


PIECES = ((0, None), (1, 0), (1, 1))
ORDER = (
    "pS", "ySo", "xFo", "pF", "sib", "ySp", "z0", "xS1o", "yS2o", "xS3o", "yF1o", "xF2o", "xFp", "z1", "yS2p",
    "yF3o", "yF2o", "xS0o", "z2", "xS2o", "xF2p", "xS23o", "xS2p", "xS1p", "yF1p", "xS0p", "xS3p", "yF2p",
    "xS20o", "xS22p", "yF22o", "xS21p", "yF21p", "xS22o", "xS20p", "xS21o", "xS23p", "yF22p", "s0", "yF3p",
    "yF23o", "JSo", "yF21o", "JF2o", "yF23p", "yL", "yE", "s1", "JS0", "JF20", "JS1", "yF0p", "JF1o", "JF21",
    "JF3o", "yL2", "JF10", "JF31", "yE2", "JF30", "s2", "JF11", "yF20p", "JF22", "JS2", "JF12", "JF32",
    "JT10", "JT00", "JTo0", "JT22", "JTo1", "JT11", "JT01",
)


def span(rows):
    return pl.ds(rows[0], rows[1] - rows[0])


def kernel(doubles_hbm, singles_hbm, b_ref, out_ref, a, own, other, c, acc, outer, doubles_ref, singles_ref, send_sem, recv_sem, local_sem):
    row, col = lax.axis_index("row"), lax.axis_index("col")
    zh, x, core = row // 8, lax.rem(row // 2, 4), lax.rem(row, 2)
    zl, y = col // 4, lax.rem(col, 4)
    zo = 1 - zl

    def at(dx=0, dy=0, dh=0, dl=0, dc=0):
        return (
            lax.rem(zh + dh, 2) * 8 + lax.rem(x + dx, 4) * 2 + lax.rem(core + dc, 2),
            lax.rem(zl + dl, 2) * 4 + lax.rem(y + dy, 4),
        )

    xs = [lax.rem(x + d, 4) for d in range(4)]
    ys = [lax.rem(y + d, 4) for d in range(4)]
    peers = [at(dx=1), at(dx=2), at(dx=3), at(dy=1), at(dy=3), at(dl=1), at(dh=1), at(dc=1)]

    bring = [
        pltpu.make_async_copy(doubles_hbm, doubles_ref, local_sem.at[14]),
        pltpu.make_async_copy(singles_hbm, singles_ref, local_sem.at[15]),
    ]
    for copy in bring[::-1]:
        copy.start()
    barrier = pltpu.get_barrier_semaphore()
    for peer in peers:
        pl.semaphore_signal(barrier, inc=1, device_id=peer, device_id_type=MESH)

    mine = pltpu.make_async_copy(b_ref, own.at[core], local_sem.at[0])
    mine.start()

    pairs, depth = doubles_ref.shape
    occupied = singles_ref.shape[0]
    first = (row * pairs) // occupied
    skip = lax.rem(row * pairs, occupied)
    lanes = lax.broadcasted_iota(jnp.int32, (1, depth), 1)
    bring[1].wait()
    for g in range(outer.shape[0] // occupied):
        line = singles_ref[pl.ds(jnp.minimum(first + g, occupied - 1), 1), :]
        factor = jnp.sum(jnp.where(lanes == col, line, 0.0), axis=1, keepdims=True)
        outer[pl.ds(g * occupied, occupied), :] = singles_ref[...] * factor
    bring[0].wait()
    a[x, y, zl, pl.ds(ROWS - 16, 16), :] = jnp.zeros((16, depth), jnp.bfloat16)
    for offset in range(0, occupied, math.gcd(pairs, occupied)):

        @pl.when(skip == offset)
        def _(offset=offset):
            tau = doubles_ref[...].astype(jnp.float32) + outer[pl.ds(offset, pairs), :]
            a[x, y, zl, pl.ds(0, pairs), :] = tau.astype(jnp.bfloat16)


    pl.semaphore_wait(barrier, len(peers))

    copies = []

    def send(src, dst, device):
        number = len(copies)
        copy = pltpu.make_async_remote_copy(
            src_ref=src,
            dst_ref=dst,
            send_sem=send_sem.at[number],
            recv_sem=recv_sem.at[number],
            device_id=device,
            device_id_type=MESH,
        )
        copy.start()
        copies.append(copy)
        return copy

    def send_a(index, rows, device):
        ref = a.at[index + (span(rows),)]
        return send(ref, ref, device)

    arrived = set()

    def arrive(started):
        for copy in started:
            if id(copy) not in arrived:
                arrived.add(id(copy))
                copy.wait_recv()

    def y_start(dx, lo, rows):
        index = (xs[dx], ys[0], lo)
        return [send_a(index, rows, at(dy=1)), send_a(index, rows, at(dy=3))]

    def y_pass(started, dx, lo, rows, flip):
        up, down = HALVES[rows][::-1] if flip else HALVES[rows]
        arrive(started)
        return [
            send_a((xs[dx], ys[3], lo), up, at(dy=1)),
            send_a((xs[dx], ys[1], lo), down, at(dy=3)),
        ]

    def x_start(dy, lo, rows):
        index = (xs[0], ys[dy], lo)
        return [send_a(index, rows, at(dx=1)), send_a(index, rows, at(dx=3))]

    def x_pass(started, dy, lo, rows, flip):
        up, down = HALVES[rows][::-1] if flip else HALVES[rows]
        arrive(started)
        return [
            send_a((xs[3], ys[dy], lo), up, at(dx=1)),
            send_a((xs[1], ys[dy], lo), down, at(dx=3)),
        ]

    def product(left, right, where, cols):
        total = None
        for lo in range(2):
            for yy in range(4):
                term = jnp.dot(
                    left(yy, lo),
                    right[pl.ds((lo * 4 + yy) * DEPTH, DEPTH), :],
                    preferred_element_type=jnp.float32,
                )
                total = term if total is None else total + term
        total = total.astype(jnp.bfloat16)
        at_row = 0
        for dx, rows in where:
            count = rows[1] - rows[0]
            c[dx, span(rows), cols] = total[at_row : at_row + count]
            at_row += count

    def own_terms(piece, chunks, stage):
        half, start, count = (0, 0, 512) if piece is None else (1, *columns_of(*piece))
        which = other if half else own
        width = min(count, WIDTH)

        def part_of(q, first):
            cols = pl.ds(half * 512 + start + first, width)
            total = acc[:, cols] if stage == 1 else None
            for yy, lo in chunks:
                term = jnp.dot(
                    a[x, yy, lo, span(FIRST)],
                    which[q, pl.ds(pl.multiple_of((lo * 4 + yy) * DEPTH, 16), DEPTH), pl.ds(start % WIDTH, width)],
                    preferred_element_type=jnp.float32,
                )
                total = term if total is None else total + term
            if stage:
                c[0, span(FIRST), cols] = total.astype(jnp.bfloat16)
            else:
                acc[:, cols] = total

        if piece is None:
            part_of(0, 0)
            part_of(1, WIDTH)
        else:
            part_of(piece[0], 0)
        if stage:
            send_c(0, FIRST, half, start, count)

    def columns_of(q, j):
        return (q * 256, 256) if j is None else (q * 256 + j * 128, 128)

    def block(which, q, j=None):
        ref = which.at[q]
        return ref if j is None else ref.at[:, pl.ds(j * 128, 128)]

    def first_rows(dx, right, cols):
        product(lambda yy, lo: a[xs[dx], yy, lo, span(FIRST)], right, [(dx, FIRST)], cols)

    def second_rows(right, cols):
        product(
            lambda yy, lo: jnp.concatenate([a[xs[d], yy, lo, span(SECOND)] for d in range(4)], axis=0),
            right,
            [(d, SECOND) for d in range(4)],
            cols,
        )

    results = []
    kept = []

    def send_c(dx, rows, half, start, count):
        base = (lax.rem(zh + half, 2) * 8 + x * 2) * WIDTH + start
        dst = out_ref.at[span(rows), pl.ds(pl.multiple_of(base, 128), count)]
        src = c.at[dx, span(rows), pl.ds(half * 512 + start, count)]
        if dx:
            results.append(send(src, dst, at(dx=dx)))
        else:
            copy = pltpu.make_async_copy(src, dst, local_sem.at[1 + len(kept)])
            copy.start()
            kept.append(copy)

    def own_first(dx):
        @pl.loop(0, 2)
        def _(q):
            first_rows(dx, own.at[q], pl.ds(pl.multiple_of(q * WIDTH, WIDTH), WIDTH))

        send_c(dx, FIRST, 0, 0, 512)

    def other_first(dx, q, j=None):
        start, count = (q * 256, 256) if j is None else (q * 256 + j * 128, 128)
        first_rows(dx, block(other, q, j), pl.ds(512 + start, count))
        send_c(dx, FIRST, 1, start, count)

    def own_second():
        @pl.loop(0, 2)
        def _(q):
            second_rows(own.at[q], pl.ds(pl.multiple_of(q * WIDTH, WIDTH), WIDTH))

        for dx in (2, 1, 3, 0):
            send_c(dx, SECOND, 0, 0, 512)

    def other_second(q, j=None):
        start, count = (q * 256, 256) if j is None else (q * 256 + j * 128, 128)
        second_rows(block(other, q, j), pl.ds(512 + start, count))
        for dx in (2, 1, 3, 0):
            send_c(dx, SECOND, 1, start, count)

    half = own.shape[1] // 2
    part = pl.ds(pl.multiple_of(core * half, half), half)
    lane_block = {None: pl.ds(0, WIDTH), 0: pl.ds(0, 128), 1: pl.ds(128, 128)}

    def across(q, j):
        return send(own.at[q, part, lane_block[j]], other.at[q, part, lane_block[j]], at(dh=1))

    def share(started, q, j):
        arrive([started])
        ref = other.at[q, part, lane_block[j]]
        return send(ref, ref, at(dc=1))

    done = {}
    los = {"o": zl, "p": zo}

    def need(*names):
        for name in names:
            arrive(done[name])

    def first_ready(dx, lo):
        if dx == 2:
            need("xF2" + lo)
        elif dx:
            need("xF" + lo)
        elif lo == "p":
            need("pF")

    def second_ready(dy, lo):
        if dy == 2:
            need("yS2" + lo)
        elif dy:
            need("yS" + lo)
        elif lo == "p":
            need("pS")

    def all_second():
        need("pS", "ySo", "ySp", "yS2o", "yS2p")
        for lo in "op":
            for dy in "0123":
                need("xS" + dy + lo, "xS2" + dy + lo)

    def all_first(dx):
        for lo in "op":
            if dx == 2:
                need("xF2" + lo)
            elif dx:
                need("xF" + lo)
            need("yF" + str(dx) + lo, "yF2" + str(dx) + lo)

    def columns_ready(which):
        if which == "o":
            need("sib")
        elif which == "0":
            need("z0", "s0")
        else:
            need("z1", "s1") if which == "1" else need("z2", "s2")

    def run(name):
        kind, rest = name[:2], name[2:]
        out = []
        if name == "sib":
            mine.wait()
            out = [sibling]
        elif kind == "pF":
            out = [send_a((xs[0], ys[0], zl), FIRST, at(dl=1))]
        elif kind == "pS":
            out = [send_a((xs[0], ys[0], zl), SECOND, at(dl=1))]
        elif name[0] == "z":
            need("sib")
            out = [across(*PIECES[int(name[1])])]
        elif name[0] == "s":
            out = [share(done["z" + name[1]][0], *PIECES[int(name[1])])]
        elif name in ("yE", "yL"):
            out = y_start(0, zl, EARLY if name == "yE" else LATE)
        elif name in ("yE2", "yL2"):
            need(name[:2])
            out = y_pass(done[name[:2]], 0, zl, EARLY if name == "yE2" else LATE, False)
        elif kind == "xF":
            lo = name[-1]
            if rest[0] == "2":
                out = x_pass(done["xF" + lo], 0, los[lo], FIRST, lo == "p")
            else:
                first_ready(0, lo)
                out = x_start(0, los[lo], FIRST)
        elif kind == "yF":
            lo, dx = name[-1], int(name[-2])
            if len(rest) == 3:
                out = y_pass(done["yF" + rest[1:]], dx, los[lo], FIRST, lo == "p")
            else:
                first_ready(dx, lo)
                out = y_start(dx, los[lo], FIRST)
        elif kind == "yS":
            lo = name[-1]
            if rest[0] == "2":
                out = y_pass(done["yS" + lo], 0, los[lo], SECOND, lo == "p")
            else:
                second_ready(0, lo)
                out = y_start(0, los[lo], SECOND)
        elif kind == "xS":
            lo, dy = name[-1], int(name[-2])
            if len(rest) == 3:
                out = x_pass(done["xS" + rest[1:]], dy, los[lo], SECOND, lo == "p")
            else:
                second_ready(dy, lo)
                out = x_start(dy, los[lo], SECOND)
        elif kind == "JS":
            all_second()
            columns_ready(rest)
            own_second() if rest == "o" else other_second(*PIECES["012".index(rest)])
        elif kind == "JF":
            dx = int(rest[0])
            all_first(dx)
            columns_ready(rest[1])
            own_first(dx) if rest[1] == "o" else other_first(dx, *PIECES["012".index(rest[1])])
        elif kind == "JT":
            stage = int(rest[1])
            piece = None if rest[0] == "o" else PIECES["012".index(rest[0])]
            need("pF", "yE", "yE2", "yL", "yL2", "yF0p")
            columns_ready(rest[0])
            early = [(ys[d], zl) for d in (0, 1, 3, 2)] + [(ys[d], zo) for d in (0, 1, 3)]
            final = [(ys[2], zo)]
            if stage:
                need("yF20p")
            if stage == 1:
                need("JT" + rest[0] + "0")
            own_terms(piece, (early, final, early + final)[stage], stage)
        done[name] = out

    sibling = send(b_ref, own.at[core], at(dc=1))
    for name in ORDER:
        run(name)
    for copy in kept:
        copy.wait()
    arrive(results)
    for copy in copies:
        copy.wait_send()


def on_device(doubles, singles, integrals):
    rows = doubles.shape[0]
    depth, width = integrals.shape
    padded = pl.pallas_call(
        kernel,
        out_shape=jax.ShapeDtypeStruct((ROWS, 16 * width), jnp.bfloat16),
        in_specs=[
            pl.BlockSpec(memory_space=pltpu.HBM),
            pl.BlockSpec(memory_space=pltpu.HBM),
            pl.BlockSpec(memory_space=pltpu.HBM),
        ],
        out_specs=pl.BlockSpec(memory_space=pl.ANY),
        scratch_shapes=[
            pltpu.VMEM((4, 4, 2, ROWS, DEPTH), jnp.bfloat16),
            pltpu.VMEM((2, depth, width), jnp.bfloat16),
            pltpu.VMEM((2, depth, width), jnp.bfloat16),
            pltpu.VMEM((4, ROWS, 4 * width), jnp.bfloat16),
            pltpu.VMEM((CUT, 4 * width), jnp.float32),
            pltpu.VMEM((300, DEPTH), jnp.float32),
            pltpu.VMEM(doubles.shape, doubles.dtype),
            pltpu.VMEM(singles.shape, singles.dtype),
            pltpu.SemaphoreType.DMA((128,)),
            pltpu.SemaphoreType.DMA((128,)),
            pltpu.SemaphoreType.DMA((16,)),
        ],
        compiler_params=pltpu.CompilerParams(
            collective_id=0, has_side_effects=True, vmem_limit_bytes=60 << 20
        ),
        cost_estimate=pl.CostEstimate(
            flops=2 * rows * depth * 16 * width, bytes_accessed=32 << 20, transcendentals=0
        ),
        name="ladder",
    )(doubles, singles, integrals)
    return padded[:rows]


def solution(mesh):
    return jax.shard_map(
        on_device,
        mesh=mesh,
        in_specs=(P("row", "col"), P(), P(None, ("col", "row"))),
        out_specs=P("row", "col"),
        check_vma=False,
    )
```

```python
import math

import jax
import jax.numpy as jnp
from jax import lax
from jax.experimental import pallas as pl
from jax.experimental.pallas import tpu as pltpu
from jax.sharding import PartitionSpec as P

MESH = pl.DeviceIdType.MESH
ROWS = 240
CUT = 176
DEPTH = 480
WIDTH = 256
ALL = (0, ROWS)
FIRST = (0, CUT)
SECOND = (CUT, ROWS)
EARLY = (0, 96)
LATE = (96, CUT)
HALVES = {
    FIRST: ((0, 96), (96, CUT)),
    SECOND: ((CUT, 208), (208, ROWS)),
    EARLY: ((0, 48), (48, 96)),
    LATE: ((96, 144), (144, CUT)),
}


PIECES = ((0, None), (1, 0), (1, 1))
ORDER = (
    "pS", "ySo", "xFo", "pF", "sib", "ySp", "z0", "xS1o", "yS2o", "xS3o", "yF1o", "xF2o", "xFp", "z1", "yS2p",
    "yF3o", "yF2o", "xS0o", "z2", "xS2o", "xF2p", "xS23o", "xS2p", "xS1p", "yF1p", "xS0p", "xS3p", "yF2p",
    "xS20o", "xS22p", "yF22o", "xS21p", "yF21p", "xS22o", "xS20p", "xS21o", "xS23p", "yF22p", "s0", "yF3p",
    "yF23o", "JSo", "yF21o", "JF2o", "yF23p", "yL", "yE", "s1", "JS0", "JF20", "JS1", "yF0p", "JF1o", "JF21",
    "JF3o", "yL2", "JF10", "JF31", "yE2", "JF30", "s2", "JF11", "yF20p", "JF22", "JS2", "JF12", "JF32",
    "JT10", "JT00", "JTo0", "JT22", "JTo1", "JT11", "JT01",
)


def span(rows):
    return pl.ds(rows[0], rows[1] - rows[0])


def kernel(doubles_hbm, singles_hbm, b_ref, out_ref, a, own, other, c, acc, outer, doubles_ref, singles_ref, send_sem, recv_sem, local_sem):
    row, col = lax.axis_index("row"), lax.axis_index("col")
    zh, x, core = row // 8, lax.rem(row // 2, 4), lax.rem(row, 2)
    zl, y = col // 4, lax.rem(col, 4)
    zo = 1 - zl

    def at(dx=0, dy=0, dh=0, dl=0, dc=0):
        return (
            lax.rem(zh + dh, 2) * 8 + lax.rem(x + dx, 4) * 2 + lax.rem(core + dc, 2),
            lax.rem(zl + dl, 2) * 4 + lax.rem(y + dy, 4),
        )

    xs = [lax.rem(x + d, 4) for d in range(4)]
    ys = [lax.rem(y + d, 4) for d in range(4)]
    peers = [at(dx=1), at(dx=2), at(dx=3), at(dy=1), at(dy=3), at(dl=1), at(dh=1), at(dc=1)]

    bring = [
        pltpu.make_async_copy(doubles_hbm, doubles_ref, local_sem.at[14]),
        pltpu.make_async_copy(singles_hbm, singles_ref, local_sem.at[15]),
    ]
    for copy in bring[::-1]:
        copy.start()
    barrier = pltpu.get_barrier_semaphore()
    for peer in peers:
        pl.semaphore_signal(barrier, inc=1, device_id=peer, device_id_type=MESH)

    mine = pltpu.make_async_copy(b_ref, own.at[core], local_sem.at[0])
    mine.start()

    pairs, depth = doubles_ref.shape
    occupied = singles_ref.shape[0]
    first = (row * pairs) // occupied
    skip = lax.rem(row * pairs, occupied)
    lanes = lax.broadcasted_iota(jnp.int32, (1, depth), 1)
    bring[1].wait()
    for g in range(outer.shape[0] // occupied):
        line = singles_ref[pl.ds(jnp.minimum(first + g, occupied - 1), 1), :]
        factor = jnp.sum(jnp.where(lanes == col, line, 0.0), axis=1, keepdims=True)
        outer[pl.ds(g * occupied, occupied), :] = singles_ref[...] * factor
    bring[0].wait()
    a[x, y, zl, pl.ds(ROWS - 16, 16), :] = jnp.zeros((16, depth), jnp.bfloat16)
    for offset in range(0, occupied, math.gcd(pairs, occupied)):

        @pl.when(skip == offset)
        def _(offset=offset):
            tau = doubles_ref[...].astype(jnp.float32) + outer[pl.ds(offset, pairs), :]
            a[x, y, zl, pl.ds(0, pairs), :] = tau.astype(jnp.bfloat16)


    pl.semaphore_wait(barrier, len(peers))

    copies = []

    def send(src, dst, device):
        number = len(copies)
        copy = pltpu.make_async_remote_copy(
            src_ref=src,
            dst_ref=dst,
            send_sem=send_sem.at[number],
            recv_sem=recv_sem.at[number],
            device_id=device,
            device_id_type=MESH,
        )
        copy.start()
        copies.append(copy)
        return copy

    def send_a(index, rows, device):
        ref = a.at[index + (span(rows),)]
        return send(ref, ref, device)

    arrived = set()

    def arrive(started):
        for copy in started:
            if id(copy) not in arrived:
                arrived.add(id(copy))
                copy.wait_recv()

    def y_start(dx, lo, rows):
        index = (xs[dx], ys[0], lo)
        return [send_a(index, rows, at(dy=1)), send_a(index, rows, at(dy=3))]

    def y_pass(started, dx, lo, rows, flip):
        up, down = HALVES[rows][::-1] if flip else HALVES[rows]
        arrive(started)
        return [
            send_a((xs[dx], ys[3], lo), up, at(dy=1)),
            send_a((xs[dx], ys[1], lo), down, at(dy=3)),
        ]

    def x_start(dy, lo, rows):
        index = (xs[0], ys[dy], lo)
        return [send_a(index, rows, at(dx=1)), send_a(index, rows, at(dx=3))]

    def x_pass(started, dy, lo, rows, flip):
        up, down = HALVES[rows][::-1] if flip else HALVES[rows]
        arrive(started)
        return [
            send_a((xs[3], ys[dy], lo), up, at(dx=1)),
            send_a((xs[1], ys[dy], lo), down, at(dx=3)),
        ]

    def product(left, right, where, cols):
        total = None
        for lo in range(2):
            for yy in range(4):
                term = jnp.dot(
                    left(yy, lo),
                    right[pl.ds((lo * 4 + yy) * DEPTH, DEPTH), :],
                    preferred_element_type=jnp.float32,
                )
                total = term if total is None else total + term
        total = total.astype(jnp.bfloat16)
        at_row = 0
        for dx, rows in where:
            count = rows[1] - rows[0]
            c[dx, span(rows), cols] = total[at_row : at_row + count]
            at_row += count

    def own_terms(piece, chunks, stage):
        half, start, count = (0, 0, 512) if piece is None else (1, *columns_of(*piece))
        which = other if half else own
        width = min(count, WIDTH)

        def part_of(q, first):
            cols = pl.ds(half * 512 + start + first, width)
            total = acc[:, cols] if stage == 1 else None
            for yy, lo in chunks:
                term = jnp.dot(
                    a[x, yy, lo, span(FIRST)],
                    which[q, pl.ds(pl.multiple_of((lo * 4 + yy) * DEPTH, 16), DEPTH), pl.ds(start % WIDTH, width)],
                    preferred_element_type=jnp.float32,
                )
                total = term if total is None else total + term
            if stage:
                c[0, span(FIRST), cols] = total.astype(jnp.bfloat16)
            else:
                acc[:, cols] = total

        if piece is None:
            part_of(0, 0)
            part_of(1, WIDTH)
        else:
            part_of(piece[0], 0)
        if stage:
            send_c(0, FIRST, half, start, count)

    def columns_of(q, j):
        return (q * 256, 256) if j is None else (q * 256 + j * 128, 128)

    def block(which, q, j=None):
        ref = which.at[q]
        return ref if j is None else ref.at[:, pl.ds(j * 128, 128)]

    def first_rows(dx, right, cols):
        product(lambda yy, lo: a[xs[dx], yy, lo, span(FIRST)], right, [(dx, FIRST)], cols)

    def second_rows(right, cols):
        product(
            lambda yy, lo: jnp.concatenate([a[xs[d], yy, lo, span(SECOND)] for d in range(4)], axis=0),
            right,
            [(d, SECOND) for d in range(4)],
            cols,
        )

    results = []
    kept = []

    def send_c(dx, rows, half, start, count):
        base = (lax.rem(zh + half, 2) * 8 + x * 2) * WIDTH + start
        dst = out_ref.at[span(rows), pl.ds(pl.multiple_of(base, 128), count)]
        src = c.at[dx, span(rows), pl.ds(half * 512 + start, count)]
        if dx:
            results.append(send(src, dst, at(dx=dx)))
        else:
            copy = pltpu.make_async_copy(src, dst, local_sem.at[1 + len(kept)])
            copy.start()
            kept.append(copy)

    def own_first(dx):
        @pl.loop(0, 2)
        def _(q):
            first_rows(dx, own.at[q], pl.ds(pl.multiple_of(q * WIDTH, WIDTH), WIDTH))

        send_c(dx, FIRST, 0, 0, 512)

    def other_first(dx, q, j=None):
        start, count = (q * 256, 256) if j is None else (q * 256 + j * 128, 128)
        first_rows(dx, block(other, q, j), pl.ds(512 + start, count))
        send_c(dx, FIRST, 1, start, count)

    def own_second():
        @pl.loop(0, 2)
        def _(q):
            second_rows(own.at[q], pl.ds(pl.multiple_of(q * WIDTH, WIDTH), WIDTH))

        for dx in (2, 1, 3, 0):
            send_c(dx, SECOND, 0, 0, 512)

    def other_second(q, j=None):
        start, count = (q * 256, 256) if j is None else (q * 256 + j * 128, 128)
        second_rows(block(other, q, j), pl.ds(512 + start, count))
        for dx in (2, 1, 3, 0):
            send_c(dx, SECOND, 1, start, count)

    half = own.shape[1] // 2
    lane_block = {None: pl.ds(0, WIDTH), 0: pl.ds(0, 128), 1: pl.ds(128, 128)}

    def parts_of(q, j):
        count = 2 if (q, j) == PIECES[-1] else 1
        rows = half // count
        return [pl.ds(pl.multiple_of(core * half + k * rows, rows), rows) for k in range(count)]

    def across(q, j):
        lanes = lane_block[j]
        return [send(own.at[q, rows, lanes], other.at[q, rows, lanes], at(dh=1)) for rows in parts_of(q, j)]

    def share(started, q, j):
        out = []
        for copy, rows in zip(started, parts_of(q, j)):
            arrive([copy])
            ref = other.at[q, rows, lane_block[j]]
            out.append(send(ref, ref, at(dc=1)))
        return out

    done = {}
    los = {"o": zl, "p": zo}

    def need(*names):
        for name in names:
            arrive(done[name])

    def first_ready(dx, lo):
        if dx == 2:
            need("xF2" + lo)
        elif dx:
            need("xF" + lo)
        elif lo == "p":
            need("pF")

    def second_ready(dy, lo):
        if dy == 2:
            need("yS2" + lo)
        elif dy:
            need("yS" + lo)
        elif lo == "p":
            need("pS")

    def all_second():
        need("pS", "ySo", "ySp", "yS2o", "yS2p")
        for lo in "op":
            for dy in "0123":
                need("xS" + dy + lo, "xS2" + dy + lo)

    def all_first(dx):
        for lo in "op":
            if dx == 2:
                need("xF2" + lo)
            elif dx:
                need("xF" + lo)
            need("yF" + str(dx) + lo, "yF2" + str(dx) + lo)

    def columns_ready(which):
        if which == "o":
            need("sib")
        elif which == "0":
            need("z0", "s0")
        else:
            need("z1", "s1") if which == "1" else need("z2", "s2")

    def run(name):
        kind, rest = name[:2], name[2:]
        out = []
        if name == "sib":
            mine.wait()
            out = [sibling]
        elif kind == "pF":
            out = [send_a((xs[0], ys[0], zl), FIRST, at(dl=1))]
        elif kind == "pS":
            out = [send_a((xs[0], ys[0], zl), SECOND, at(dl=1))]
        elif name[0] == "z":
            need("sib")
            out = across(*PIECES[int(name[1])])
        elif name[0] == "s":
            out = share(done["z" + name[1]], *PIECES[int(name[1])])
        elif name in ("yE", "yL"):
            out = y_start(0, zl, EARLY if name == "yE" else LATE)
        elif name in ("yE2", "yL2"):
            need(name[:2])
            out = y_pass(done[name[:2]], 0, zl, EARLY if name == "yE2" else LATE, False)
        elif kind == "xF":
            lo = name[-1]
            if rest[0] == "2":
                out = x_pass(done["xF" + lo], 0, los[lo], FIRST, lo == "p")
            else:
                first_ready(0, lo)
                out = x_start(0, los[lo], FIRST)
        elif kind == "yF":
            lo, dx = name[-1], int(name[-2])
            if len(rest) == 3:
                out = y_pass(done["yF" + rest[1:]], dx, los[lo], FIRST, lo == "p")
            else:
                first_ready(dx, lo)
                out = y_start(dx, los[lo], FIRST)
        elif kind == "yS":
            lo = name[-1]
            if rest[0] == "2":
                out = y_pass(done["yS" + lo], 0, los[lo], SECOND, lo == "p")
            else:
                second_ready(0, lo)
                out = y_start(0, los[lo], SECOND)
        elif kind == "xS":
            lo, dy = name[-1], int(name[-2])
            if len(rest) == 3:
                out = x_pass(done["xS" + rest[1:]], dy, los[lo], SECOND, lo == "p")
            else:
                second_ready(dy, lo)
                out = x_start(dy, los[lo], SECOND)
        elif kind == "JS":
            all_second()
            columns_ready(rest)
            own_second() if rest == "o" else other_second(*PIECES["012".index(rest)])
        elif kind == "JF":
            dx = int(rest[0])
            all_first(dx)
            columns_ready(rest[1])
            own_first(dx) if rest[1] == "o" else other_first(dx, *PIECES["012".index(rest[1])])
        elif kind == "JT":
            stage = int(rest[1])
            piece = None if rest[0] == "o" else PIECES["012".index(rest[0])]
            need("pF", "yE", "yE2", "yL", "yL2", "yF0p")
            columns_ready(rest[0])
            early = [(ys[d], zl) for d in (0, 1, 3, 2)] + [(ys[d], zo) for d in (0, 1, 3)]
            final = [(ys[2], zo)]
            if stage:
                need("yF20p")
            if stage == 1:
                need("JT" + rest[0] + "0")
            own_terms(piece, (early, final, early + final)[stage], stage)
        done[name] = out

    sibling = send(b_ref, own.at[core], at(dc=1))
    for name in ORDER:
        run(name)
    for copy in kept:
        copy.wait()
    arrive(results)
    for copy in copies:
        copy.wait_send()


def on_device(doubles, singles, integrals):
    rows = doubles.shape[0]
    depth, width = integrals.shape
    padded = pl.pallas_call(
        kernel,
        out_shape=jax.ShapeDtypeStruct((ROWS, 16 * width), jnp.bfloat16),
        in_specs=[
            pl.BlockSpec(memory_space=pltpu.HBM),
            pl.BlockSpec(memory_space=pltpu.HBM),
            pl.BlockSpec(memory_space=pltpu.HBM),
        ],
        out_specs=pl.BlockSpec(memory_space=pl.ANY),
        scratch_shapes=[
            pltpu.VMEM((4, 4, 2, ROWS, DEPTH), jnp.bfloat16),
            pltpu.VMEM((2, depth, width), jnp.bfloat16),
            pltpu.VMEM((2, depth, width), jnp.bfloat16),
            pltpu.VMEM((4, ROWS, 4 * width), jnp.bfloat16),
            pltpu.VMEM((CUT, 4 * width), jnp.float32),
            pltpu.VMEM((300, DEPTH), jnp.float32),
            pltpu.VMEM(doubles.shape, doubles.dtype),
            pltpu.VMEM(singles.shape, singles.dtype),
            pltpu.SemaphoreType.DMA((128,)),
            pltpu.SemaphoreType.DMA((128,)),
            pltpu.SemaphoreType.DMA((16,)),
        ],
        compiler_params=pltpu.CompilerParams(
            collective_id=0, has_side_effects=True, vmem_limit_bytes=60 << 20
        ),
        cost_estimate=pl.CostEstimate(
            flops=2 * rows * depth * 16 * width, bytes_accessed=32 << 20, transcendentals=0
        ),
        name="ladder",
    )(doubles, singles, integrals)
    return padded[:rows]


def solution(mesh):
    return jax.shard_map(
        on_device,
        mesh=mesh,
        in_specs=(P("row", "col"), P(), P(None, ("col", "row"))),
        out_specs=P("row", "col"),
        check_vma=False,
    )
```
